32 devices in a mesh: rep: 8 (over z, x), tp: 4 (over y, core).
Axes of the slice: x: 2, y: 2, z: 4, core: 2. Of those that a mesh axis runs over, the one named last changes fastest.
Arguments:
- hidden: bfloat16 [16384, 8192], P('rep', 'tp'), may hold values from -0.0625 to 0.0625
- target: bfloat16 [16384, 1024], P('rep'), may hold values from -6 to 6
- inner_weight: bfloat16 [8, 8192, 1024], P('rep', 'tp'), as said below
- first_moment: float32 [8, 8192, 1024], P('rep', 'tp'), may hold values from -1.5 to 1.5
- second_moment: float32 [8, 8192, 1024], P('rep', 'tp'), may hold values from 0.001 to 0.01
- anchor: float32 [4, 2048, 1024], P('tp', 'rep')
- outer_momentum: float32 [4, 2048, 1024], P('tp', 'rep'), may hold values from -1.5 to 1.5
Outputs:
- fragment: bfloat16 [8192, 1024], P('tp')
- momentum_new: float32 [4, 2048, 1024], P('tp', 'rep')
The draws below stay inside these ranges and needn't reach their ends.
Inputs may be any that keep to these rules, and one draw needn't show every extreme that they name: `inner_weight`: each replica's inner weights are the anchor plus a drift of their own.
All inputs are finite; a program needn't handle non-finite values.
Results may differ from the reference program's by a relative error of at most 0.0017.
Values may be sent and summed in bfloat16 or wider, within the bound.
A program may use at most 128 MiB of HBM per device.

```python
import math
import jax
import jax.numpy as jnp
from jax import lax

D = 8192
KVW = 1024
TOK = 2048
REPS = 8
ROWS = 2048
TOKENS = 16384
N_TP = 4


def shared_base(key):
    inner_key = jax.random.fold_in(key, 11)
    base = jax.random.normal(inner_key, (D, KVW), jnp.float32)
    return base


def draw_anchor(key, part):
    return shared_base(key).reshape(N_TP, ROWS, KVW)


def draw_inner_weight(key, part):
    base = shared_base(key)
    drift = 0.1 * jax.random.normal(jax.random.fold_in(key, 12), (REPS, D, KVW), jnp.float32)
    return (base[None, :, :] + drift).astype(jnp.bfloat16)


def levels(key, shape, split, least, top_value):
    factor_of = 1.0
    for axis_at, parts in split:
        heights = jax.random.uniform(jax.random.fold_in(jax.random.fold_in(key, 6), axis_at), (parts,), jnp.float32, least / len(split), top_value / len(split))
        factor_of = factor_of * jnp.repeat(jnp.exp(heights), shape[axis_at] // parts).reshape((-1,) + (1,) * (len(shape) - 1 - axis_at))
    return factor_of


def centred(key, extent, deviation, most, split=(), held_as=jnp.bfloat16):
    values = jax.random.normal(key, extent, jnp.float32) * deviation
    if len(split) > 0:
        values = levels(key, extent, split, -0.22, 0.18) * values
    return jnp.clip(values, min=-most, max=most).astype(held_as)


def setup_inputs(seed: int = 0) -> dict:
    key_of = jax.random.split(jax.random.key(seed), 8)
    return {
        "hidden": centred(key_of[0], (TOKENS, D), D ** -0.5, 0.0625, ((0, 8), (1, 4))),
        "target": centred(key_of[1], (TOKENS, KVW), 1.0, 6.0, ((0, 8),)),
        "inner_weight": draw_inner_weight(jax.random.fold_in(key_of[7], 71), 0),
        "first_moment": centred(key_of[3], (REPS, D, KVW), 0.1, 1.5, ((0, 8), (1, 4)), jnp.float32),
        "second_moment": jnp.clip(jnp.exp(math.log(0.01) - 2.30258502 * jax.random.uniform(key_of[4], (REPS, D, KVW), jnp.float32) ** levels(key_of[4], (REPS, D, KVW), ((0, 8), (1, 4)), -0.2, 0.2)), 0.001, 0.01),
        "anchor": draw_anchor(jax.random.fold_in(key_of[7], 71), 0),
        "outer_momentum": centred(key_of[6], (N_TP, ROWS, KVW), 0.1, 1.5, ((0, 4), (1, 8)), jnp.float32),
    }


beta_one = 0.9
beta_two = 0.999
inner_rate = 0.2
decay_rate = 0.1
outer_rate = 0.7
outer_mu = 0.9
adam_eps = 1e-08

def replica_step(total, inputs):
    rows, goal, weight, moment_a, moment_b = inputs
    shards_h = jnp.transpose(rows.reshape(TOK, N_TP, ROWS), (1, 0, 2))
    shards_w = weight.reshape(N_TP, ROWS, KVW)

    def add_group(acc, pair):
        piece_h, piece_w = pair
        part = jnp.dot(piece_h, piece_w, preferred_element_type=jnp.float32).astype(jnp.bfloat16)
        part = lax.optimization_barrier(part)
        return (acc + part.astype(jnp.float32), None)
    output, unused = lax.scan(add_group, jnp.zeros((TOK, KVW), jnp.float32), (shards_h, shards_w))
    residual = (output - goal.astype(jnp.float32)).astype(jnp.bfloat16)
    grad = lax.dot_general(rows, residual, (((0,), (0,)), ((), ())), preferred_element_type=jnp.float32)
    moment_one = beta_one * moment_a + (1.0 - beta_one) * grad
    moment_two = beta_two * moment_b + (1.0 - beta_two) * grad * grad
    corr_one = 1.0 - beta_one ** 3
    corr_two = 1.0 - beta_two ** 3
    weight_f = weight.astype(jnp.float32)
    step_dir = moment_one / corr_one / (jnp.sqrt(moment_two / corr_two) + adam_eps)
    updated = weight_f - inner_rate * (step_dir + decay_rate * weight_f)
    return (total + updated, None)

def reference(hidden, target, inner_weight, first_moment, second_moment, anchor, outer_momentum):
    rows = hidden.reshape(REPS, TOK, D)
    goals = target.reshape(REPS, TOK, KVW)
    total, unused = lax.scan(replica_step, jnp.zeros((D, KVW), jnp.float32), (rows, goals, inner_weight, first_moment, second_moment))
    replica_mean = total / REPS
    anchor_flat = anchor.reshape(D, KVW)
    momentum_flat = outer_momentum.reshape(D, KVW)
    delta = anchor_flat - replica_mean
    momentum_new = outer_mu * momentum_flat + delta
    fragment = (anchor_flat - outer_rate * (delta + outer_mu * momentum_new)).astype(jnp.bfloat16)
    return (fragment, momentum_new.reshape(N_TP, ROWS, KVW))
```

```python
import functools

import jax
import jax.numpy as jnp
from jax import lax
from jax.experimental import pallas as pl
from jax.experimental.pallas import tpu as pltpu
from jax.sharding import PartitionSpec as P

beta_one = 0.9
beta_two = 0.999
inner_rate = 0.2
decay_rate = 0.1
outer_rate = 0.7
outer_mu = 0.9
adam_eps = 1e-08

MESH = pl.DeviceIdType.MESH
bf16 = jnp.bfloat16
f32 = jnp.float32


def kernel(n, n_tp, C, W, cnt, RB,
           hidden, target, weight, fm, sm, anchor, om,
           frag_out, mom_out,
           h, wv, goal, pv, prx, psum, yrx, res, anch, dl, rrx, frag, m1, m2, af, omv, mv,
           h_sem, w_sem, g_sem, a_sem, o_sem, m_sem, v_sem, out_sem, mo_sem,
           cs, cr, ys, yr, gs, gr, xs, xr, as_, ar, rs, rr, fs, fr):
    m = n_tp // 2
    KA, KB = n // 2, n // 2 - 1
    me = lax.axis_index("rep")
    tp = lax.axis_index("tp")
    core = lax.rem(tp, 2)
    chip = tp // 2
    mate = tp + 1 - 2 * core
    zz = me // 2
    pos = jnp.where(lax.rem(me, 2) == 0, zz, n - 1 - zz)

    def at_pos(p):
        p = lax.rem(p + 2 * n, n)
        return jnp.where(p < n // 2, 2 * p, 2 * (n - 1 - p) + 1)

    def peer(j):
        return lax.rem(chip + j, m) * 2 + core

    def cols(c):
        return pl.ds(pl.multiple_of(c * W, W), W)

    def h_copy(i):
        return pltpu.make_async_copy(hidden.at[pl.ds(i * cnt, cnt)], h.at[pl.ds(i * cnt, cnt)], h_sem.at[i])

    def w_copy(c):
        return pltpu.make_async_copy(weight.at[0, :, cols(c)], wv.at[c], w_sem.at[c])

    def goal_copy():
        return pltpu.make_async_copy(target.at[pl.ds(pl.multiple_of(tp * cnt, cnt), cnt)], goal, g_sem)

    def a_copy(c):
        return pltpu.make_async_copy(anchor.at[0, :, cols(c)], af.at[c], a_sem.at[c])

    def o_copy(c):
        return pltpu.make_async_copy(om.at[0, :, cols(c)], omv.at[c], o_sem.at[c])

    def m_copy(c, s):
        return pltpu.make_async_copy(fm.at[0, :, cols(c)], m1.at[s], m_sem.at[s])

    def v_copy(c, s):
        return pltpu.make_async_copy(sm.at[0, :, cols(c)], m2.at[s], v_sem.at[s])

    def out_copy(c, b):
        return pltpu.make_async_copy(
            frag.at[c, b], frag_out.at[pl.ds(pl.multiple_of(b * RB, RB), RB), cols(c)], out_sem.at[c, b])

    def mo_copy(c):
        return pltpu.make_async_copy(mv.at[c], mom_out.at[0, :, cols(c)], mo_sem.at[c])

    def remote(src, dst, ss, rsem, dev):
        return pltpu.make_async_remote_copy(
            src_ref=src, dst_ref=dst, send_sem=ss, recv_sem=rsem, device_id=dev, device_id_type=MESH)

    def core_copy(c):
        return remote(pv.at[c, :, 1 - core], prx.at[c], cs.at[c], cr.at[c], {"tp": mate})

    def y_copy(c, j):
        return remote(psum.at[c, j - 1], yrx.at[c, j - 1], ys.at[c, j - 1], yr.at[c, j - 1], {"tp": peer(j)})

    def g_copy(c, j):
        return remote(res.at[c, tp], res.at[c, tp], gs.at[c, j - 1], gr.at[c, j - 1], {"tp": peer(j)})

    def x_copy(c, j):
        src = lax.rem(chip + m - j, m) * 2 + core
        return remote(res.at[c, src], res.at[c, src], xs.at[c, j], xr.at[c, j], {"tp": mate})

    def x_recv(c, j):
        src = lax.rem(chip + m - j, m) * 2 + 1 - core
        return remote(res.at[c, src], res.at[c, src], xs.at[c, j], xr.at[c, j], {"tp": mate})

    def g_recv(c, j):
        src = lax.rem(chip + m - j, m) * 2 + core
        return remote(res.at[c, src], res.at[c, src], gs.at[c, j - 1], gr.at[c, j - 1], {"tp": peer(j)})

    def way(c, side):
        d = 1 - 2 * lax.rem(c, 2)
        return d if side == 0 else -d

    def hops(side):
        return KA if side == 0 else KB

    def slot(side, k):
        return k - 1 if side == 0 else KA + k - 1

    def gather(buf, ss, rsem, c, side, k, recv=False):
        d = way(c, side)
        b = at_pos(pos - d * (k if recv else k - 1))
        i = slot(side, k)
        return remote(buf.at[c, b], buf.at[c, b], ss.at[c, i], rsem.at[c, i], {"rep": at_pos(pos + d)})

    def scatter(c, side, k):
        d = way(c, side)
        b = at_pos(pos + d * (hops(side) - k + 1))
        i = slot(side, k)
        return remote(dl.at[c, b], rrx.at[c, i], rs.at[c, i], rr.at[c, i], {"rep": at_pos(pos + d)})

    for c in range(C):
        a_copy(c).start()
    w_copy(0).start()
    for i in range(n_tp):
        h_copy(i).start()
    goal_copy().start()
    for c in range(1, C):
        w_copy(c).start()
    for s in range(2):
        m_copy(s, s).start()
        v_copy(s, s).start()
    for c in range(C):
        o_copy(c).start()

    barrier = pltpu.get_barrier_semaphore()
    pl.semaphore_signal(barrier, inc=1, device_id={"tp": mate}, device_id_type=MESH)
    for j in range(1, m):
        pl.semaphore_signal(barrier, inc=1, device_id={"tp": peer(j)}, device_id_type=MESH)
    for d in (1, -1):
        pl.semaphore_signal(barrier, inc=1, device_id={"rep": at_pos(pos + d)}, device_id_type=MESH)
    for c in range(C):
        a_copy(c).wait()
        anch[c, me] = af[c].astype(bf16)
    pl.semaphore_wait(barrier, m + 2)

    def anchor_first(c):
        gather(anch, as_, ar, c, 0, 1).start()
        gather(anch, as_, ar, c, 1, 1).start()

    def anchor_hop(k, c):
        for side in (0, 1):
            if k <= hops(side):
                gather(anch, as_, ar, c, side, k, True).wait_recv()
                if k < hops(side):
                    gather(anch, as_, ar, c, side, k + 1).start()

    def forward(c):
        w_copy(c).wait()

        def tile(i, carry):
            @pl.when(c == 0)
            def _():
                h_copy(i).wait()
            pv[c, i // 2, lax.rem(i, 2)] = jnp.dot(
                h[pl.ds(pl.multiple_of(i * cnt, cnt), cnt)], wv[c], preferred_element_type=f32).astype(bf16)
            return carry
        lax.fori_loop(0, n_tp, tile, 0)
        core_copy(c).start()

    def pair(c, to):
        return pv[c, to, core].astype(f32) + prx[c, to].astype(f32)

    def chip_sum(c):
        core_copy(c).wait_recv()
        for j in range(1, m):
            psum[c, j - 1] = pair(c, lax.rem(chip + j, m)).astype(bf16)
            y_copy(c, j).start()

    def residual(c):
        @pl.when(c == 0)
        def _():
            goal_copy().wait()
        total = pair(c, chip)
        for j in range(1, m):
            y_copy(c, j).wait_recv()
            total += yrx[c, j - 1].astype(f32)
        res[c, tp] = (total - goal[:, cols(c)].astype(f32)).astype(bf16)
        for j in range(1, m):
            g_copy(c, j).start()
        x_copy(c, 0).start()

    def spread(c):
        for j in range(1, m):
            g_recv(c, j).wait_recv()
            x_copy(c, j).start()

    GB = max(RB, 128)
    sub = GB // RB
    corr_one = 1.0 - beta_one**3
    corr_two = 1.0 - beta_two**3

    def block(c, i):
        d = way(c, 0)
        half = i // 2
        step = jnp.where(lax.rem(i, 2) == 0, d * (KA - half), -d * (KB - half))
        b = at_pos(pos + step)
        s = lax.rem(c, 2)
        hs = h[:, pl.ds(pl.multiple_of((b // sub) * GB, GB), GB)]
        g = lax.dot_general(hs, res[c].reshape(n_tp * cnt, W), (((0,), (0,)), ((), ())),
                            preferred_element_type=f32)
        if sub > 1:
            part = g[:RB]
            for q in range(1, sub):
                part = jnp.where(lax.rem(b, sub) == q, g[q * RB:(q + 1) * RB], part)
            g = part
        rows = pl.ds(pl.multiple_of(b * RB, RB), RB)
        one = beta_one * m1[s, rows] + (1.0 - beta_one) * g
        two = beta_two * m2[s, rows] + (1.0 - beta_two) * g * g
        wf = wv[c, rows].astype(f32)
        direction = one * (1.0 / corr_one) / (jnp.sqrt(two * (1.0 / corr_two)) + adam_eps)
        updated = wf - inner_rate * (direction + decay_rate * wf)
        dl[c, b] = (anch[c, b].astype(f32) - updated).astype(bf16)

    Q = n // 2

    def inner(c, j):
        s = lax.rem(c, 2)

        @pl.when(j == 0)
        def _():
            for q in range(m):
                x_recv(c, q).wait_recv()
            m_copy(c, s).wait()
            v_copy(c, s).wait()

        def two_blocks(i, carry):
            block(c, j * 2 + i)
            return carry
        lax.fori_loop(0, 2, two_blocks, 0)

        @pl.when(j == 0)
        def _():
            scatter(c, 0, 1).start()
            scatter(c, 1, 1).start()

        @pl.when((j == Q - 1) & (c + 2 < C))
        def _():
            m_copy(c + 2, s).start()
            v_copy(c + 2, s).start()

    def reduce_hop(k, c):
        for side in (0, 1):
            if k <= hops(side):
                scatter(c, side, k).wait_recv()
                if k < hops(side):
                    b = at_pos(pos + way(c, side) * (hops(side) - k))
                    dl[c, b] = (dl[c, b].astype(f32) + rrx[c, slot(side, k)].astype(f32)).astype(bf16)
                    scatter(c, side, k + 1).start()

    def outer(c):
        reduce_hop(KA, c)
        o_copy(c).wait()
        total = dl[c, me].astype(f32) + rrx[c, slot(0, KA)].astype(f32) + rrx[c, slot(1, KB)].astype(f32)
        base = af[c]
        delta = (base - anch[c, me].astype(f32)) + total * (1.0 / n)
        new = outer_mu * omv[c] + delta
        mv[c] = new
        frag[c, me] = (base - outer_rate * (delta + outer_mu * new)).astype(bf16)
        gather(frag, fs, fr, c, 0, 1).start()
        gather(frag, fs, fr, c, 1, 1).start()
        mo_copy(c).start()
        out_copy(c, me).start()

    def frag_hop(k, c):
        for side in (0, 1):
            if k <= hops(side):
                gather(frag, fs, fr, c, side, k, True).wait_recv()
                if k < hops(side):
                    gather(frag, fs, fr, c, side, k + 1).start()
                out_copy(c, at_pos(pos - way(c, side) * k)).start()

    stages = []
    S = Q
    start = 4
    for k in range(1, KA + 1):
        stages.append((k, 2, functools.partial(anchor_hop, k)))
    stages.append((0, 2, anchor_first))
    HS = 1
    for k in range(1, KA):
        stages.append((start + 1 + HS * k, S, functools.partial(reduce_hop, k)))
    last = max(start + 1 + HS * KA, start + Q)
    stages.append((last, S, outer))
    for k in range(1, KA + 1):
        stages.append((last + HS * k, S, functools.partial(frag_hop, k)))
    stages.append((3, S, spread))
    stages.append((2, S, residual))
    stages.append((1, S, chip_sum))
    stages.append((0, S, forward))

    ticks = max(o + s * (C - 1) for o, s, _ in stages) + 1

    def tick(t, carry):
        for off, stride, stage in stages:
            q = t - off

            @pl.when((q >= 0) & (lax.rem(q + stride * ticks, stride) == 0) & (q < stride * C))
            def _():
                stage(q // stride)
        q = t - start

        @pl.when((q >= 0) & (q < Q * C))
        def _():
            inner(q // Q, lax.rem(q, Q))
        return carry
    lax.fori_loop(0, ticks, tick, 0)

    def drain(c, carry):
        core_copy(c).wait_send()
        for j in range(1, m):
            y_copy(c, j).wait_send()
            g_copy(c, j).wait_send()
        for j in range(m):
            x_copy(c, j).wait_send()
        for side in (0, 1):
            for k in range(1, hops(side) + 1):
                gather(anch, as_, ar, c, side, k).wait_send()
                scatter(c, side, k).wait_send()
                gather(frag, fs, fr, c, side, k).wait_send()
        mo_copy(c).wait()
        for b in range(n):
            out_copy(c, b).wait()
        return carry
    lax.fori_loop(0, C, drain, 0)


def local(C, hidden, target, inner_weight, first_moment, second_moment, anchor, outer_momentum):
    n, n_tp = lax.axis_size("rep"), lax.axis_size("tp")
    tok, rows = hidden.shape
    kvw = target.shape[1]
    W = kvw // C
    cnt = tok // n_tp
    RB = rows // n
    m = n_tp // 2
    any_ = pl.BlockSpec(memory_space=pl.ANY)
    dma = pltpu.SemaphoreType.DMA
    V = pltpu.VMEM
    scratch = [
        V((tok, rows), bf16), V((C, rows, W), bf16), V((cnt, kvw), bf16),
        V((C, m, 2, cnt, W), bf16), V((C, m, cnt, W), bf16), V((C, m - 1, cnt, W), bf16),
        V((C, m - 1, cnt, W), bf16), V((C, n_tp, cnt, W), bf16),
        V((C, n, RB, W), bf16), V((C, n, RB, W), bf16), V((C, n - 1, RB, W), bf16), V((C, n, RB, W), bf16),
        V((2, rows, W), f32), V((2, rows, W), f32),
        V((C, RB, W), f32), V((C, RB, W), f32), V((C, RB, W), f32),
        dma((n_tp,)), dma((C,)), dma, dma((C,)), dma((C,)), dma((2,)), dma((2,)), dma((C, n)), dma((C,)),
        dma((C,)), dma((C,)), dma((C, m - 1)), dma((C, m - 1)), dma((C, m - 1)), dma((C, m - 1)),
        dma((C, m)), dma((C, m)),
        dma((C, n - 1)), dma((C, n - 1)), dma((C, n - 1)), dma((C, n - 1)), dma((C, n - 1)), dma((C, n - 1)),
    ]
    return pl.pallas_call(
        functools.partial(kernel, n, n_tp, C, W, cnt, RB),
        out_shape=(jax.ShapeDtypeStruct((rows, kvw), bf16),
                   jax.ShapeDtypeStruct(anchor.shape, f32)),
        in_specs=[any_] * 7,
        out_specs=(any_, any_),
        scratch_shapes=scratch,
        compiler_params=pltpu.CompilerParams(
            collective_id=0, has_side_effects=True, vmem_limit_bytes=62 * 2**20),
        cost_estimate=pl.CostEstimate(
            flops=4 * tok * rows * kvw, bytes_accessed=40 * 2**20, transcendentals=rows * kvw),
    )(hidden, target, inner_weight, first_moment, second_moment, anchor, outer_momentum)


def solution(mesh):
    placed = (
        P("rep", "tp"),
        P("rep", None),
        P("rep", "tp", None),
        P("rep", "tp", None),
        P("rep", "tp", None),
        P("tp", "rep", None),
        P("tp", "rep", None),
    )
    return jax.shard_map(
        functools.partial(local, 4),
        mesh=mesh,
        in_specs=placed,
        out_specs=(P("tp", None), P("tp", "rep", None)),
        check_vma=False,
    )
```

```python
import functools

import jax
import jax.numpy as jnp
from jax import lax
from jax.experimental import pallas as pl
from jax.experimental.pallas import tpu as pltpu
from jax.sharding import PartitionSpec as P

beta_one = 0.9
beta_two = 0.999
inner_rate = 0.2
decay_rate = 0.1
outer_rate = 0.7
outer_mu = 0.9
adam_eps = 1e-08

MESH = pl.DeviceIdType.MESH
bf16 = jnp.bfloat16
f32 = jnp.float32


def kernel(n, n_tp, C, W, cnt, RB,
           hidden, target, weight, fm, sm, anchor, om,
           frag_out, mom_out,
           h, wv, goal, pv, prx, psum, yrx, res, anch, dl, rrx, frag, m1, m2, af, omv, mv,
           h_sem, w_sem, g_sem, a_sem, o_sem, m_sem, v_sem, out_sem, mo_sem,
           cs, cr, ys, yr, gs, gr, xs, xr, as_, ar, rs, rr, fs, fr):
    m = n_tp // 2
    KA, KB = n // 2, n // 2 - 1
    me = lax.axis_index("rep")
    tp = lax.axis_index("tp")
    core = lax.rem(tp, 2)
    chip = tp // 2
    mate = tp + 1 - 2 * core
    zz = me // 2
    pos = jnp.where(lax.rem(me, 2) == 0, zz, n - 1 - zz)

    def at_pos(p):
        p = lax.rem(p + 2 * n, n)
        return jnp.where(p < n // 2, 2 * p, 2 * (n - 1 - p) + 1)

    def peer(j):
        return lax.rem(chip + j, m) * 2 + core

    def cols(c):
        return pl.ds(pl.multiple_of(c * W, W), W)

    def h_copy(i):
        return pltpu.make_async_copy(hidden.at[pl.ds(i * cnt, cnt)], h.at[pl.ds(i * cnt, cnt)], h_sem.at[i])

    def w_copy(c):
        return pltpu.make_async_copy(weight.at[0, :, cols(c)], wv.at[c], w_sem.at[c])

    def goal_copy():
        return pltpu.make_async_copy(target.at[pl.ds(pl.multiple_of(tp * cnt, cnt), cnt)], goal, g_sem)

    def a_copy(c):
        return pltpu.make_async_copy(anchor.at[0, :, cols(c)], af.at[c], a_sem.at[c])

    def o_copy(c):
        return pltpu.make_async_copy(om.at[0, :, cols(c)], omv.at[c], o_sem.at[c])

    def m_copy(c, s):
        return pltpu.make_async_copy(fm.at[0, :, cols(c)], m1.at[s], m_sem.at[s])

    def v_copy(c, s):
        return pltpu.make_async_copy(sm.at[0, :, cols(c)], m2.at[s], v_sem.at[s])

    def out_copy(c, b):
        return pltpu.make_async_copy(
            frag.at[c, b], frag_out.at[pl.ds(pl.multiple_of(b * RB, RB), RB), cols(c)], out_sem.at[c, b])

    def mo_copy(c):
        return pltpu.make_async_copy(mv.at[c], mom_out.at[0, :, cols(c)], mo_sem.at[c])

    def remote(src, dst, ss, rsem, dev):
        return pltpu.make_async_remote_copy(
            src_ref=src, dst_ref=dst, send_sem=ss, recv_sem=rsem, device_id=dev, device_id_type=MESH)

    def core_copy(c):
        return remote(pv.at[c, :, 1 - core], prx.at[c], cs.at[c], cr.at[c], {"tp": mate})

    def y_copy(c, j):
        return remote(psum.at[c, j - 1], yrx.at[c, j - 1], ys.at[c, j - 1], yr.at[c, j - 1], {"tp": peer(j)})

    def g_copy(c, j):
        return remote(res.at[c, tp], res.at[c, tp], gs.at[c, j - 1], gr.at[c, j - 1], {"tp": peer(j)})

    def x_copy(c, j):
        src = lax.rem(chip + m - j, m) * 2 + core
        return remote(res.at[c, src], res.at[c, src], xs.at[c, j], xr.at[c, j], {"tp": mate})

    def x_recv(c, j):
        src = lax.rem(chip + m - j, m) * 2 + 1 - core
        return remote(res.at[c, src], res.at[c, src], xs.at[c, j], xr.at[c, j], {"tp": mate})

    def g_recv(c, j):
        src = lax.rem(chip + m - j, m) * 2 + core
        return remote(res.at[c, src], res.at[c, src], gs.at[c, j - 1], gr.at[c, j - 1], {"tp": peer(j)})

    def way(c, side):
        d = 1 - 2 * lax.rem(c, 2)
        return d if side == 0 else -d

    def hops(side):
        return KA if side == 0 else KB

    def slot(side, k):
        return k - 1 if side == 0 else KA + k - 1

    def gather(buf, ss, rsem, c, side, k, recv=False):
        d = way(c, side)
        b = at_pos(pos - d * (k if recv else k - 1))
        i = slot(side, k)
        return remote(buf.at[c, b], buf.at[c, b], ss.at[c, i], rsem.at[c, i], {"rep": at_pos(pos + d)})

    def scatter(c, side, k):
        d = way(c, side)
        b = at_pos(pos + d * (hops(side) - k + 1))
        i = slot(side, k)
        return remote(dl.at[c, b], rrx.at[c, i], rs.at[c, i], rr.at[c, i], {"rep": at_pos(pos + d)})

    for c in range(C):
        a_copy(c).start()
    w_copy(0).start()
    for i in range(n_tp):
        h_copy(i).start()
    goal_copy().start()
    for c in range(1, C):
        w_copy(c).start()
    for s in range(2):
        m_copy(s, s).start()
        v_copy(s, s).start()
    for c in range(C):
        o_copy(c).start()

    barrier = pltpu.get_barrier_semaphore()
    pl.semaphore_signal(barrier, inc=1, device_id={"tp": mate}, device_id_type=MESH)
    for j in range(1, m):
        pl.semaphore_signal(barrier, inc=1, device_id={"tp": peer(j)}, device_id_type=MESH)
    for d in (1, -1):
        pl.semaphore_signal(barrier, inc=1, device_id={"rep": at_pos(pos + d)}, device_id_type=MESH)
    for c in range(C):
        a_copy(c).wait()
        anch[c, me] = af[c].astype(bf16)
    pl.semaphore_wait(barrier, m + 2)

    def anchor_first(c):
        gather(anch, as_, ar, c, 0, 1).start()
        gather(anch, as_, ar, c, 1, 1).start()

    def anchor_hop(k, c):
        for side in (0, 1):
            if k <= hops(side):
                gather(anch, as_, ar, c, side, k, True).wait_recv()
                if k < hops(side):
                    gather(anch, as_, ar, c, side, k + 1).start()

    def forward(c):
        w_copy(c).wait()

        def tile(i, carry):
            @pl.when(c == 0)
            def _():
                h_copy(i).wait()
            pv[c, i // 2, lax.rem(i, 2)] = jnp.dot(
                h[pl.ds(pl.multiple_of(i * cnt, cnt), cnt)], wv[c], preferred_element_type=f32).astype(bf16)
            return carry
        lax.fori_loop(0, n_tp, tile, 0)
        core_copy(c).start()

    def pair(c, to):
        return pv[c, to, core].astype(f32) + prx[c, to].astype(f32)

    def chip_sum(c):
        core_copy(c).wait_recv()
        for j in range(1, m):
            psum[c, j - 1] = pair(c, lax.rem(chip + j, m)).astype(bf16)
            y_copy(c, j).start()

    def residual(c):
        @pl.when(c == 0)
        def _():
            goal_copy().wait()
        total = pair(c, chip)
        for j in range(1, m):
            y_copy(c, j).wait_recv()
            total += yrx[c, j - 1].astype(f32)
        res[c, tp] = (total - goal[:, cols(c)].astype(f32)).astype(bf16)
        for j in range(1, m):
            g_copy(c, j).start()
        x_copy(c, 0).start()

    def spread(c):
        for j in range(1, m):
            g_recv(c, j).wait_recv()
            x_copy(c, j).start()

    GB = max(RB, 128)
    sub = GB // RB
    corr_one = 1.0 - beta_one**3
    corr_two = 1.0 - beta_two**3
    keep = 1.0 - inner_rate * decay_rate

    def block(c, i):
        d = way(c, 0)
        half = i // 2
        step = jnp.where(lax.rem(i, 2) == 0, d * (KA - half), -d * (KB - half))
        b = at_pos(pos + step)
        s = lax.rem(c, 2)
        hs = h[:, pl.ds(pl.multiple_of((b // sub) * GB, GB), GB)]
        g = lax.dot_general(hs, res[c].reshape(n_tp * cnt, W), (((0,), (0,)), ((), ())),
                            preferred_element_type=f32)
        if sub > 1:
            part = g[:RB]
            for q in range(1, sub):
                part = jnp.where(lax.rem(b, sub) == q, g[q * RB:(q + 1) * RB], part)
            g = part
        rows = pl.ds(pl.multiple_of(b * RB, RB), RB)
        one = beta_one * m1[s, rows] + (1.0 - beta_one) * g
        two = beta_two * m2[s, rows] + (1.0 - beta_two) * g * g
        wf = wv[c, rows].astype(f32)
        direction = one * (1.0 / corr_one) / (jnp.sqrt(two * (1.0 / corr_two)) + adam_eps)
        updated = wf - inner_rate * (direction + decay_rate * wf)
        dl[c, b] = (keep * anch[c, b].astype(f32) - updated).astype(bf16)

    Q = n // 2
    parts = 1
    size = n // parts

    def inner(c, j):
        s = lax.rem(c, 2)

        @pl.when(j == 0)
        def _():
            for q in range(m):
                x_recv(c, q).wait_recv()
            m_copy(c, s).wait()
            v_copy(c, s).wait()

        def one_block(i, carry):
            block(c, j * size + i)

            @pl.when((j == 0) & (i == 0))
            def _():
                scatter(c, 0, 1).start()

            @pl.when((j == 0) & (i == 1))
            def _():
                scatter(c, 1, 1).start()
            return carry
        lax.fori_loop(0, size, one_block, 0)

        @pl.when((j == parts - 1) & (c + 2 < C))
        def _():
            m_copy(c + 2, s).start()
            v_copy(c + 2, s).start()

    def reduce_hop(k, c):
        for side in (0, 1):
            if k <= hops(side):
                scatter(c, side, k).wait_recv()
                if k < hops(side):
                    b = at_pos(pos + way(c, side) * (hops(side) - k))
                    dl[c, b] = (dl[c, b].astype(f32) + rrx[c, slot(side, k)].astype(f32)).astype(bf16)
                    scatter(c, side, k + 1).start()

    def outer(c):
        reduce_hop(KA, c)
        o_copy(c).wait()
        total = dl[c, me].astype(f32) + rrx[c, slot(0, KA)].astype(f32) + rrx[c, slot(1, KB)].astype(f32)
        base = af[c]
        delta = (base - keep * anch[c, me].astype(f32)) + total * (1.0 / n)
        new = outer_mu * omv[c] + delta
        mv[c] = new
        frag[c, me] = (base - outer_rate * (delta + outer_mu * new)).astype(bf16)
        gather(frag, fs, fr, c, 0, 1).start()
        gather(frag, fs, fr, c, 1, 1).start()
        mo_copy(c).start()
        out_copy(c, me).start()

    def frag_hop(k, c):
        for side in (0, 1):
            if k <= hops(side):
                gather(frag, fs, fr, c, side, k, True).wait_recv()
                if k < hops(side):
                    gather(frag, fs, fr, c, side, k + 1).start()
                out_copy(c, at_pos(pos - way(c, side) * k)).start()

    S = parts
    start = max(4, KA)

    def after(k):
        return start + 1 + max(k - 1, min(k, Q - 1) * parts // Q)

    tp_stages = [(3, S, spread), (2, S, residual), (1, S, chip_sum), (0, S, forward)]
    stages = [(k, S, functools.partial(anchor_hop, k)) for k in range(1, KA + 1)]
    stages += [(0, S, anchor_first)]
    ring = [(after(k), S, functools.partial(reduce_hop, k)) for k in range(1, KA)]
    last = after(KA)
    ring += [(last, S, outer)]
    ring += [(last + k, S, functools.partial(frag_hop, k)) for k in range(1, KA + 1)]
    stages = tp_stages[::-1] + stages + ring

    ticks = max(o + s * (C - 1) for o, s, _ in stages) + 1

    def tick(t, carry):
        for off, stride, stage in stages:
            q = t - off

            @pl.when((q >= 0) & (lax.rem(q + stride * ticks, stride) == 0) & (q < stride * C))
            def _():
                stage(q // stride)
        q = t - start

        @pl.when((q >= 0) & (q < parts * C))
        def _():
            inner(q // parts, lax.rem(q, parts))
        return carry
    lax.fori_loop(0, ticks, tick, 0)

    def drain(c, carry):
        core_copy(c).wait_send()
        for j in range(1, m):
            y_copy(c, j).wait_send()
            g_copy(c, j).wait_send()
        for j in range(m):
            x_copy(c, j).wait_send()
        for side in (0, 1):
            for k in range(1, hops(side) + 1):
                gather(anch, as_, ar, c, side, k).wait_send()
                scatter(c, side, k).wait_send()
                gather(frag, fs, fr, c, side, k).wait_send()
        mo_copy(c).wait()
        for b in range(n):
            out_copy(c, b).wait()
        return carry
    lax.fori_loop(0, C, drain, 0)


def local(C, hidden, target, inner_weight, first_moment, second_moment, anchor, outer_momentum):
    n, n_tp = lax.axis_size("rep"), lax.axis_size("tp")
    tok, rows = hidden.shape
    kvw = target.shape[1]
    W = kvw // C
    cnt = tok // n_tp
    RB = rows // n
    m = n_tp // 2
    any_ = pl.BlockSpec(memory_space=pl.ANY)
    dma = pltpu.SemaphoreType.DMA
    V = pltpu.VMEM
    scratch = [
        V((tok, rows), bf16), V((C, rows, W), bf16), V((cnt, kvw), bf16),
        V((C, m, 2, cnt, W), bf16), V((C, m, cnt, W), bf16), V((C, m - 1, cnt, W), bf16),
        V((C, m - 1, cnt, W), bf16), V((C, n_tp, cnt, W), bf16),
        V((C, n, RB, W), bf16), V((C, n, RB, W), bf16), V((C, n - 1, RB, W), bf16), V((C, n, RB, W), bf16),
        V((2, rows, W), f32), V((2, rows, W), f32),
        V((C, RB, W), f32), V((C, RB, W), f32), V((C, RB, W), f32),
        dma((n_tp,)), dma((C,)), dma, dma((C,)), dma((C,)), dma((2,)), dma((2,)), dma((C, n)), dma((C,)),
        dma((C,)), dma((C,)), dma((C, m - 1)), dma((C, m - 1)), dma((C, m - 1)), dma((C, m - 1)),
        dma((C, m)), dma((C, m)),
        dma((C, n - 1)), dma((C, n - 1)), dma((C, n - 1)), dma((C, n - 1)), dma((C, n - 1)), dma((C, n - 1)),
    ]
    return pl.pallas_call(
        functools.partial(kernel, n, n_tp, C, W, cnt, RB),
        out_shape=(jax.ShapeDtypeStruct((rows, kvw), bf16),
                   jax.ShapeDtypeStruct(anchor.shape, f32)),
        in_specs=[any_] * 7,
        out_specs=(any_, any_),
        scratch_shapes=scratch,
        compiler_params=pltpu.CompilerParams(
            collective_id=0, has_side_effects=True, vmem_limit_bytes=62 * 2**20),
        cost_estimate=pl.CostEstimate(
            flops=4 * tok * rows * kvw, bytes_accessed=40 * 2**20, transcendentals=rows * kvw),
    )(hidden, target, inner_weight, first_moment, second_moment, anchor, outer_momentum)


def solution(mesh):
    placed = (
        P("rep", "tp"),
        P("rep", None),
        P("rep", "tp", None),
        P("rep", "tp", None),
        P("rep", "tp", None),
        P("tp", "rep", None),
        P("tp", "rep", None),
    )
    return jax.shard_map(
        functools.partial(local, 4),
        mesh=mesh,
        in_specs=placed,
        out_specs=(P("tp", None), P("tp", "rep", None)),
        check_vma=False,
    )
```
